32 devices in a mesh: dp: 4 (over y, core), tensor: 8 (over z, x).
Axes of the slice: x: 2, y: 2, z: 4, core: 2. Of those that a mesh axis runs over, the one named last changes fastest.
Arguments:
- hidden: bfloat16 [1024, 14336], P('dp', 'tensor'), may hold values from -6 to 6
- residual: bfloat16 [1024, 8192], P('tensor', 'dp'), may hold values from -6 to 6
- master: float32 [14336, 8192], P('tensor', 'dp'), may hold values from -0.046875 to 0.046875
- moment: float32 [14336, 8192], P('tensor', 'dp'), may hold values from -0.00021362305 to 0.00021362305
- second: float32 [14336, 8192], P('tensor', 'dp'), as said below
- gain: float32 [8192], P('dp'), may hold values from 0.5 to 1.5
- head: float32 [8192], P('dp')
- lengths: int32 [4, 2], replicated, may hold values from 32 to 128, as said below
- labels: int32 [4], replicated, may hold values from 0 to 1
Outputs:
- new_master: float32 [14336, 8192], P('tensor', 'dp')
- new_moment: float32 [14336, 8192], P('tensor', 'dp')
- new_second: float32 [14336, 8192], P('tensor', 'dp')
- loss: float32 [], replicated
The draws below stay inside these ranges and needn't reach their ends.
Inputs may be any that keep to these rules, and one draw needn't show every extreme that they name: `lengths`: some sequence has exactly 128 valid tokens in every draw; every sequence has at least 32. `second`: Positive.
All inputs are finite; a program needn't handle non-finite values.
Results may differ from the reference program's by a relative error of at most 0.015.
Values may be sent and summed in bfloat16 or wider, within the bound.
A program may use at most 192 MiB of HBM per device.

```python
import jax
import jax.numpy as jnp
from jax import lax

D = 8192
FF = 14336
LEN = 128
STEP = 100
PAIRS = 4
TOKENS = 1024
N_TENSOR = 8


def draw_lengths(key, part):
    first_key, second_key = jax.random.split(key)
    values = jax.random.randint(first_key, (PAIRS * 2,), LEN // 4, LEN + 1)
    where_full = jax.random.randint(second_key, (), 0, PAIRS * 2)
    values = jnp.where(jnp.arange(PAIRS * 2) == where_full, LEN, values)
    return values.reshape(PAIRS, 2).astype(jnp.int32)


def head_pattern(key):
    sub_key = jax.random.fold_in(key, 11)
    pattern = jnp.clip(jax.random.normal(sub_key, (D,), jnp.float32), -4.0, 4.0)
    return pattern


def draw_head(key, part):
    return (head_pattern(key) * (16.0 / D)).astype(jnp.float32)


def draw_residual(key, part):
    pattern = head_pattern(key)
    noise_key = jax.random.fold_in(key, 23)
    along_key = jax.random.fold_in(key, 37)
    noise = jnp.clip(jax.random.normal(noise_key, (TOKENS, D), jnp.float32), -4.0, 4.0)
    along = jax.random.uniform(along_key, (TOKENS, 1), jnp.float32, -0.8, 0.8)
    values = jnp.clip(noise + along * pattern[None, :], -6.0, 6.0)
    return values.astype(jnp.bfloat16)


def draw_second(key, part):
    sub_key = jax.random.fold_in(key, 5)
    logs = jax.random.uniform(sub_key, (FF, D), jnp.float32, jnp.log(0.3), jnp.log(3.0))
    return (jnp.exp(logs) / (float(D) * float(D))).astype(jnp.float32)


def place_ends(array, rng, low, high):
    shape = array.shape
    index_at = [jax.random.randint(jax.random.fold_in(rng, axis), (), 0, shape[axis]) for axis in range(len(shape))]
    array = array.at[tuple(index_at)].set(low)
    longest = shape.index(max(shape))
    index_at[longest] = (index_at[longest] + 1) % shape[longest]
    return array.at[tuple(index_at)].set(high)


def steps_of(rng, extent, shards, least, high):
    factor_of, own = 1.0, jax.random.fold_in(rng, 6)
    for axis_at, blocks in shards:
        heights = jnp.exp(jax.random.uniform(jax.random.fold_in(own, axis_at), (blocks,), jnp.float32, least / len(shards), high / len(shards)))
        factor_of = factor_of * jnp.repeat(heights, extent[axis_at] // blocks).reshape([-1 if axis == axis_at else 1 for axis in range(len(extent))])
    return factor_of


def gaussian(stream_key, extent, width, bound, cuts=(), dtype=jnp.bfloat16):
    entries = width * jax.random.normal(stream_key, extent, jnp.float32)
    if cuts:
        entries = entries * steps_of(stream_key, extent, cuts, -0.22, 0.18)
    return jnp.clip(entries, -bound, bound).astype(dtype)


def setup_inputs(seed: int = 0) -> dict:
    keys = jax.random.split(jax.random.key(seed), 10)
    hidden = gaussian(keys[0], (TOKENS, FF), 1.0, 6.0, ((0, 4), (1, 8)))
    residual = draw_residual(jax.random.fold_in(keys[9], 71), 0)
    master = gaussian(keys[2], (FF, D), FF ** -0.5, 0.046875, ((0, 8), (1, 4)), jnp.float32)
    moment = gaussian(keys[3], (FF, D), (11 * D * D) ** -0.5, 0.00021362305, ((0, 8), (1, 4)), jnp.float32)
    second = draw_second(jax.random.fold_in(keys[9], 71), 0)
    gain = jnp.clip(1.0 + 0.1 * jax.random.normal(keys[5], (D,), jnp.float32), 0.5, 1.5)
    head = draw_head(jax.random.fold_in(keys[9], 71), 0)
    lengths = draw_lengths(jax.random.fold_in(keys[9], 71), 0)
    labels = place_ends(jax.random.randint(keys[8], (PAIRS,), 0, 2), jax.random.fold_in(keys[8], 1), 0, 1).astype(jnp.int32)
    return {"hidden": hidden, "residual": residual, "master": master, "moment": moment, "second": second, "gain": gain, "head": head, "lengths": lengths, "labels": labels}


EPS_NORM = 1e-05

def reference(hidden, residual, master, moment, second, gain, head, lengths, labels):
    weights = master.astype(jnp.bfloat16)
    block_ff = FF // N_TENSOR
    block_rows = TOKENS // N_TENSOR
    resid = residual.astype(jnp.float32)

    def add_block(total, index):
        cols = lax.dynamic_slice_in_dim(hidden, index * block_ff, block_ff, 1)
        wrows = lax.dynamic_slice_in_dim(weights, index * block_ff, block_ff, 0)
        part = jnp.dot(cols, wrows, preferred_element_type=jnp.float32)
        own = lax.dynamic_slice_in_dim(part, index * block_rows, block_rows, 0)
        own = own + lax.dynamic_slice_in_dim(resid, index * block_rows, block_rows, 0)
        part = lax.dynamic_update_slice_in_dim(part, own, index * block_rows, 0)
        rounded = lax.optimization_barrier(part.astype(jnp.bfloat16))
        return (total + rounded.astype(jnp.float32), None)
    stream, _ = lax.scan(add_block, jnp.zeros((TOKENS, D), jnp.float32), jnp.arange(N_TENSOR).astype(jnp.int32))
    w_vec = gain * head
    row_ids = jnp.arange(TOKENS).astype(jnp.int32)
    seq_ids = row_ids // LEN
    pos = row_ids % LEN
    lens_flat = lengths.reshape(-1)
    len_row = lens_flat[seq_ids]
    valid = pos < len_row
    ss = lax.optimization_barrier(jnp.sum(stream * stream, 1))
    hy = lax.optimization_barrier(jnp.sum(stream * w_vec[None, :], 1))
    rstd = lax.rsqrt(ss / D + EPS_NORM)
    score = rstd * hy
    seq_total = jax.ops.segment_sum(jnp.where(valid, score, 0.0), seq_ids, 2 * PAIRS)
    reward = (seq_total / lens_flat.astype(jnp.float32)).reshape(PAIRS, 2)
    chosen = jnp.where(labels == 1, reward[:, 1], reward[:, 0])
    other = jnp.where(labels == 1, reward[:, 0], reward[:, 1])
    margin = chosen - other
    loss = jnp.sum(jax.nn.softplus(-margin))
    sig = jax.nn.sigmoid(-margin)
    first = jnp.where(labels == 0, -sig, sig)
    dreward = jnp.stack([first, -first], 1).reshape(-1)
    coef = jnp.where(valid, dreward[seq_ids] / len_row.astype(jnp.float32), 0.0)
    cotangent = (coef[:, None] * (rstd[:, None] * w_vec[None, :] - (hy * rstd ** 3 / D)[:, None] * stream)).astype(jnp.bfloat16)
    grad = jnp.dot(hidden.T, cotangent, preferred_element_type=jnp.float32)
    new_moment = 0.9 * moment + 0.1 * grad
    new_second = 0.95 * second + 0.05 * grad * grad
    m_hat = new_moment / (1.0 - 0.9 ** STEP)
    v_hat = new_second / (1.0 - 0.95 ** STEP)
    new_master = master - 0.001 * (m_hat / (jnp.sqrt(v_hat) + 1e-08) + 0.1 * master)
    return (new_master, new_moment, new_second, loss)
```

```python
import functools

import jax
import jax.numpy as jnp
from jax import lax
from jax.experimental import pallas as pl
from jax.experimental.pallas import tpu as pltpu
from jax.sharding import PartitionSpec as P

LEN = 128
STEP = 100
EPS_NORM = 1e-05
MIB = 1024 * 1024


def update_kernel(h_ref, s_ref, a_ref, b_ref, w_ref, p_ref, m_ref, v_ref, po_ref, mo_ref, vo_ref, cot):
    @pl.when(pl.program_id(0) == 0)
    def _():
        def fill(i, carry):
            rows = pl.ds(pl.multiple_of(i * 64, 64), 64)
            value = a_ref[rows, :] * w_ref[...] - b_ref[rows, :] * s_ref[rows, :].astype(jnp.float32)
            cot[rows, :] = value.astype(jnp.bfloat16)
            return carry

        lax.fori_loop(0, cot.shape[0] // 64, fill, 0)

    h = h_ref[...]
    wide = cot.shape[1]
    step = 512
    for c in range(wide // step):
        cols = slice(c * step, (c + 1) * step)
        grad = lax.dot_general(
            h, cot[:, cols], (((0,), (0,)), ((), ())), preferred_element_type=jnp.float32
        )
        moment = 0.9 * m_ref[:, cols] + 0.1 * grad
        second = 0.95 * v_ref[:, cols] + 0.05 * grad * grad
        mo_ref[:, cols] = moment
        vo_ref[:, cols] = second
        m_hat = moment * (1.0 / (1.0 - 0.9**STEP))
        v_hat = second * (1.0 / (1.0 - 0.95**STEP))
        master = p_ref[:, cols]
        po_ref[:, cols] = master - 0.001 * (m_hat / (jnp.sqrt(v_hat) + 1e-08) + 0.1 * master)


def update(hidden, stream, a, b, w, master, moment, second):
    tokens, ff = hidden.shape
    wide = stream.shape[1]
    tile = 128
    state = pl.BlockSpec((tile, wide), lambda i: (i, 0))
    whole = lambda x: pl.BlockSpec(x.shape, lambda i: (0, 0), pipeline_mode=pl.Buffered(1))
    out = jax.ShapeDtypeStruct(master.shape, jnp.float32)
    return pl.pallas_call(
        update_kernel,
        grid=(ff // tile,),
        in_specs=[pl.BlockSpec((tokens, tile), lambda i: (0, i))]
        + [whole(x) for x in (stream, a, b, w)]
        + [state] * 3,
        out_specs=[state] * 3,
        out_shape=[out] * 3,
        scratch_shapes=[pltpu.VMEM(stream.shape, jnp.bfloat16)],
        compiler_params=pltpu.CompilerParams(vmem_limit_bytes=48 * MIB),
        cost_estimate=pl.CostEstimate(
            flops=2 * tokens * ff * wide, bytes_accessed=24 * ff * wide, transcendentals=ff * wide
        ),
    )(hidden, stream, a, b, w, master, moment, second)


def row_terms(stream, w, lengths, labels, full_width):
    value = stream.astype(jnp.float32)
    sums = jnp.stack([jnp.sum(value * value, 1), jnp.sum(value * w[None, :], 1)])
    squares, product = lax.psum(sums, "dp")
    lens = lengths.reshape(-1)
    lens_f = lens.astype(jnp.float32)[:, None]
    valid = jnp.arange(LEN, dtype=jnp.int32)[None, :] < lens[:, None]
    squares = squares.reshape(-1, LEN)
    product = product.reshape(-1, LEN)
    rstd = lax.rsqrt(squares / full_width + EPS_NORM)
    total = jnp.sum(jnp.where(valid, rstd * product, 0.0), 1)
    reward = (total / lens_f[:, 0]).reshape(-1, 2)
    chosen = jnp.where(labels == 1, reward[:, 1], reward[:, 0])
    other = jnp.where(labels == 1, reward[:, 0], reward[:, 1])
    margin = chosen - other
    loss = jnp.sum(jax.nn.softplus(-margin))
    sig = jax.nn.sigmoid(-margin)
    first = jnp.where(labels == 0, -sig, sig)
    dreward = jnp.stack([first, -first], 1).reshape(-1, 1)
    coef = jnp.where(valid, dreward / lens_f, 0.0)
    a = (coef * rstd).reshape(-1, 1)
    b = (coef * (product * rstd**3 / full_width)).reshape(-1, 1)
    return a, b, loss


def per_device(dp, tensor, hidden, residual, master, moment, second, gain, head, lengths, labels):
    t_index = lax.axis_index("tensor")
    block_rows = residual.shape[0]
    gathered = lax.all_gather(hidden, "dp", axis=0, tiled=True)
    partial_value = jnp.dot(gathered, master.astype(jnp.bfloat16), preferred_element_type=jnp.float32)
    row_start = t_index * block_rows
    own = lax.dynamic_slice_in_dim(partial_value, row_start, block_rows, 0) + residual.astype(
        jnp.float32
    )
    term = lax.dynamic_update_slice_in_dim(partial_value, own, row_start, 0).astype(jnp.bfloat16)
    part = lax.psum_scatter(term, "tensor", scatter_dimension=0, tiled=True)
    stream = lax.all_gather(part, "tensor", axis=0, tiled=True)
    w = gain * head
    a, b, loss = row_terms(stream, w, lengths, labels, w.shape[0] * dp)
    new_master, new_moment, new_second = update(
        gathered, stream, a, b, w[None, :], master, moment, second
    )
    return new_master, new_moment, new_second, loss


def solution(mesh):
    state = P("tensor", "dp")
    return jax.shard_map(
        functools.partial(per_device, mesh.shape["dp"], mesh.shape["tensor"]),
        mesh=mesh,
        in_specs=(P("dp", "tensor"), state, state, state, state, P("dp"), P("dp"), P(), P()),
        out_specs=(state, state, state, P()),
        check_vma=False,
    )
```

```python
import functools

import jax
import jax.numpy as jnp
from jax import lax
from jax.experimental import pallas as pl
from jax.experimental.pallas import tpu as pltpu
from jax.sharding import PartitionSpec as P

LEN = 128
STEP = 100
EPS_NORM = 1e-05
MIB = 1024 * 1024
MESH = pl.DeviceIdType.MESH


def update_kernel(h_ref, s_ref, a_ref, b_ref, w_ref, p_ref, m_ref, v_ref, po_ref, mo_ref, vo_ref, cot):
    @pl.when(pl.program_id(0) == 0)
    def _():
        def fill(i, carry):
            rows = pl.ds(pl.multiple_of(i * 64, 64), 64)
            value = a_ref[rows, :] * w_ref[...] - b_ref[rows, :] * s_ref[rows, :].astype(jnp.float32)
            cot[rows, :] = value.astype(jnp.bfloat16)
            return carry

        lax.fori_loop(0, cot.shape[0] // 64, fill, 0)

    h = h_ref[...]
    wide = cot.shape[1]
    step = 512
    for c in range(wide // step):
        cols = slice(c * step, (c + 1) * step)
        grad = lax.dot_general(
            h, cot[:, cols], (((0,), (0,)), ((), ())), preferred_element_type=jnp.float32
        )
        moment = 0.9 * m_ref[:, cols] + 0.1 * grad
        second = 0.95 * v_ref[:, cols] + 0.05 * grad * grad
        mo_ref[:, cols] = moment
        vo_ref[:, cols] = second
        m_hat = moment * (1.0 / (1.0 - 0.9**STEP))
        v_hat = second * (1.0 / (1.0 - 0.95**STEP))
        master = p_ref[:, cols]
        po_ref[:, cols] = master - 0.001 * (m_hat / (jnp.sqrt(v_hat) + 1e-08) + 0.1 * master)


def update(hidden, stream, a, b, w, master, moment, second):
    tokens, ff = hidden.shape
    wide = stream.shape[1]
    tile = 128
    state = pl.BlockSpec((tile, wide), lambda i: (i, 0))
    whole = lambda x: pl.BlockSpec(x.shape, lambda i: (0, 0), pipeline_mode=pl.Buffered(1))
    out = jax.ShapeDtypeStruct(master.shape, jnp.float32)
    return pl.pallas_call(
        update_kernel,
        grid=(ff // tile,),
        in_specs=[pl.BlockSpec((tokens, tile), lambda i: (0, i))]
        + [whole(x) for x in (stream, a, b, w)]
        + [state] * 3,
        out_specs=[state] * 3,
        out_shape=[out] * 3,
        scratch_shapes=[pltpu.VMEM(stream.shape, jnp.bfloat16)],
        compiler_params=pltpu.CompilerParams(vmem_limit_bytes=48 * MIB),
        cost_estimate=pl.CostEstimate(
            flops=2 * tokens * ff * wide, bytes_accessed=24 * ff * wide, transcendentals=ff * wide
        ),
    )(hidden, stream, a, b, w, master, moment, second)


def row_terms(stream, w, lengths, labels, full_width):
    value = stream.astype(jnp.float32)
    sums = jnp.stack([jnp.sum(value * value, 1), jnp.sum(value * w[None, :], 1)])
    squares, product = lax.psum(sums, "dp")
    lens = lengths.reshape(-1)
    lens_f = lens.astype(jnp.float32)[:, None]
    valid = jnp.arange(LEN, dtype=jnp.int32)[None, :] < lens[:, None]
    squares = squares.reshape(-1, LEN)
    product = product.reshape(-1, LEN)
    rstd = lax.rsqrt(squares / full_width + EPS_NORM)
    total = jnp.sum(jnp.where(valid, rstd * product, 0.0), 1)
    reward = (total / lens_f[:, 0]).reshape(-1, 2)
    chosen = jnp.where(labels == 1, reward[:, 1], reward[:, 0])
    other = jnp.where(labels == 1, reward[:, 0], reward[:, 1])
    margin = chosen - other
    loss = jnp.sum(jax.nn.softplus(-margin))
    sig = jax.nn.sigmoid(-margin)
    first = jnp.where(labels == 0, -sig, sig)
    dreward = jnp.stack([first, -first], 1).reshape(-1, 1)
    coef = jnp.where(valid, dreward / lens_f, 0.0)
    a = (coef * rstd).reshape(-1, 1)
    b = (coef * (product * rstd**3 / full_width)).reshape(-1, 1)
    return a, b, loss


def forward_kernel(dp, n, lanes, hidden, residual, master, hid_out, stream_out, hid, stream, partial,
                   stage, weights, early_in, early_out, late_in, late_out, stage_sem, own_sem,
                   block_send, block_recv, ring_send, ring_recv, out_sem):
    f32, bf16 = jnp.float32, jnp.bfloat16
    d, t = lax.axis_index("dp"), lax.axis_index("tensor")
    pairs = dp // 2
    q, core = d // 2, d % 2
    rows, wide = hidden.shape[0], master.shape[1]
    lane_cols, chunk = wide // lanes, rows // n
    mate = 2 * q + 1 - core

    def seat(place):
        place = lax.rem(place + n, n)
        return jnp.where(place < n // 2, 2 * place, 2 * (n - 1 - place) + 1)

    place = jnp.where(t % 2 == 0, t // 2, n - 1 - t // 2)
    right, left = seat(place + 1), seat(place - 1)

    def block(k):
        return 2 * lax.rem(q - k // 2 + pairs, pairs) + lax.rem(core + k, 2)

    def block_rows(k):
        return pl.ds(pl.multiple_of(block(k) * rows, rows), rows)

    depth = stage_rows(master.shape[0])
    pieces = master.shape[0] // depth

    def stage_copy(i):
        at = pl.ds(pl.multiple_of(i * depth, depth), depth)
        return pltpu.make_async_copy(master.at[at], stage.at[at], stage_sem.at[i])

    for i in range(pieces):
        stage_copy(i).start()
    own_copy = pltpu.make_async_copy(hidden, hid.at[block_rows(0)], own_sem)
    own_copy.start()

    barrier = pltpu.get_barrier_semaphore()
    greeted = [{"tensor": right}, {"tensor": left}, {"dp": mate}]
    greeted += [{"dp": 2 * lax.rem(q + j, pairs) + core} for j in range(1, pairs)]
    for other in greeted:
        pl.semaphore_signal(barrier, inc=1, device_id=other, device_id_type=MESH)
    pl.semaphore_wait(barrier, len(greeted))

    def block_copy(k):
        if k == 1 or k % 2 == 0:
            src, at = hidden, block_rows(0)
        else:
            src, at = hid.at[block_rows(k - 1)], block_rows(k - 1)
        to = mate if k % 2 else 2 * lax.rem(q + k // 2, pairs) + core
        return pltpu.make_async_remote_copy(
            src_ref=src, dst_ref=hid.at[at], send_sem=block_send.at[k - 1], recv_sem=block_recv.at[k - 1],
            device_id={"dp": to}, device_id_type=MESH,
        )

    def block_wait(k):
        pltpu.make_async_remote_copy(
            src_ref=hidden, dst_ref=hid.at[block_rows(k)], send_sem=block_send.at[k - 1],
            recv_sem=block_recv.at[k - 1], device_id={"dp": mate}, device_id_type=MESH,
        ).wait_recv()

    for k in [1] + list(range(2, dp, 2)):
        block_copy(k).start()

    def to_weights(i, carry):
        stage_copy(i).wait()
        at = pl.ds(pl.multiple_of(i * depth, depth), depth)
        weights[at, :] = stage[at, :].astype(bf16)
        return carry

    lax.fori_loop(0, pieces, to_weights, 0)

    def multiply(k):
        at = block_rows(k)

        def tile(c, carry):
            cols = pl.ds(pl.multiple_of(c * 256, 256), 256)
            partial[k, :, cols] = jnp.dot(hid[at, :], weights[:, cols], preferred_element_type=f32)
            return carry

        lax.fori_loop(0, wide // 256, tile, 0)
        res_rows = residual.shape[0]

        @pl.when(block(k) == t * res_rows // rows)
        def _():
            own = pl.ds(pl.multiple_of(lax.rem(t * res_rows, rows), res_rows), res_rows)
            partial[k, own, :] += residual[...].astype(f32)

    sets = [(0, 0, 2, early_in, early_out), (1, 2, dp - 2, late_in, late_out)]

    def chunk_at(lane, offset):
        mirrored = place if lane % 2 == 0 else n - place
        index = lax.rem(mirrored + offset + 2 * n, n)
        return pl.ds(pl.multiple_of(index * chunk, chunk), chunk)

    def ring_copy(which, lane, step, src, dst):
        return pltpu.make_async_remote_copy(
            src_ref=src, dst_ref=dst, send_sem=ring_send.at[which, lane, step],
            recv_sem=ring_recv.at[which, lane, step],
            device_id={"tensor": right if lane % 2 == 0 else left}, device_id_type=MESH,
        )

    def sum_copy(group, lane, step):
        which, first, count, arrive, leave = group
        return ring_copy(which, lane, step, leave.at[lane, step], arrive.at[lane, step])

    def share_copy(group, lane, step, offset):
        which, first, count, arrive, leave = group
        at = stream.at[pl.ds(first, count), chunk_at(lane, offset), pl.ds(lane * lane_cols, lane_cols)]
        return ring_copy(which, lane, n - 1 + step, at, at)

    def own_part(group, lane, offset):
        which, first, count, arrive, leave = group
        return partial[pl.ds(first, count), chunk_at(lane, offset), pl.ds(lane * lane_cols, lane_cols)]

    def begin(group):
        for lane in range(lanes):
            group[4][lane, 0] = own_part(group, lane, 0).astype(bf16)
            sum_copy(group, lane, 0).start()

    def add_step(group, step):
        for lane in range(lanes):
            sum_copy(group, lane, step - 1).wait_recv()
            total = group[3][lane, step - 1].astype(f32) + own_part(group, lane, -step)
            group[4][lane, step] = total.astype(bf16)
            sum_copy(group, lane, step).start()

    def turn(group):
        which, first, count, arrive, leave = group
        for lane in range(lanes):
            sum_copy(group, lane, n - 2).wait_recv()
            total = arrive[lane, n - 2].astype(f32) + own_part(group, lane, 1)
            cols = pl.ds(lane * lane_cols, lane_cols)
            stream[pl.ds(first, count), chunk_at(lane, 1), cols] = total.astype(bf16)
            share_copy(group, lane, 0, 1).start()

    def share_step(group, step):
        for lane in range(lanes):
            share_copy(group, lane, step - 1, 1 - step).wait_recv()
            share_copy(group, lane, step, 1 - step).start()

    def finish(group):
        for lane in range(lanes):
            share_copy(group, lane, n - 2, 2 - n).wait_recv()

    def sent(group):
        for lane in range(lanes):

            def wait(step, carry):
                sum_copy(group, lane, step).wait_send()
                share_copy(group, lane, step, 1 - step).wait_send()
                return carry

            lax.fori_loop(0, n - 1, wait, 0)

    def result_copy(k):
        return pltpu.make_async_copy(stream.at[k], stream_out.at[block_rows(k)], out_sem.at[k])

    early, late = sets
    own_copy.wait()
    multiply(0)
    block_wait(1)
    multiply(1)
    begin(early)

    def early_sums(step, carry):
        add_step(early, step)
        return carry

    lax.fori_loop(1, n - 1, early_sums, 0)
    turn(early)
    for k in range(2, dp, 2):
        block_wait(k)
        block_copy(k + 1).start()
    for k in range(2, dp):
        if k % 2:
            block_wait(k)
        multiply(k)
    hid_copy = pltpu.make_async_copy(hid, hid_out, out_sem.at[dp])
    hid_copy.start()
    begin(late)

    def both(step, carry):
        share_step(early, step)
        add_step(late, step)
        return carry

    lax.fori_loop(1, n - 1, both, 0)
    finish(early)
    turn(late)
    for k in range(2):
        result_copy(k).start()

    def late_shares(step, carry):
        share_step(late, step)
        return carry

    lax.fori_loop(1, n - 1, late_shares, 0)
    finish(late)
    for k in range(2, dp):
        result_copy(k).start()
    for k in range(1, dp):
        block_copy(k).wait_send()
    sent(early)
    sent(late)
    for k in range(dp):
        result_copy(k).wait()
    hid_copy.wait()


def stage_rows(depth):
    return 128 if depth % 128 == 0 else depth


def forward(dp, n, hidden, residual, master):
    rows, depth = hidden.shape
    wide = master.shape[1]
    tokens = rows * dp
    lanes = 4
    chunk, lane_cols = rows // n, wide // lanes
    bf16 = jnp.bfloat16
    slots = lambda count: pltpu.VMEM((lanes, n - 1, count, chunk, lane_cols), bf16)
    dma = pltpu.SemaphoreType.DMA
    vmem = pl.BlockSpec(memory_space=pltpu.VMEM)
    hbm = pl.BlockSpec(memory_space=pl.ANY)
    return pl.pallas_call(
        functools.partial(forward_kernel, dp, n, lanes),
        in_specs=[vmem, vmem, hbm],
        out_specs=[hbm, hbm],
        out_shape=[
            jax.ShapeDtypeStruct((tokens, depth), bf16),
            jax.ShapeDtypeStruct((tokens, wide), bf16),
        ],
        scratch_shapes=[
            pltpu.VMEM((tokens, depth), bf16),
            pltpu.VMEM((dp, rows, wide), bf16),
            pltpu.VMEM((dp, rows, wide), jnp.float32),
            pltpu.VMEM((depth, wide), jnp.float32),
            pltpu.VMEM((depth, wide), bf16),
            slots(2), slots(2), slots(dp - 2), slots(dp - 2),
            dma((depth // stage_rows(depth),)),
            dma,
            dma((dp - 1,)), dma((dp - 1,)),
            dma((2, lanes, 2 * n - 2)), dma((2, lanes, 2 * n - 2)),
            dma((dp + 1,)),
        ],
        compiler_params=pltpu.CompilerParams(
            collective_id=0, has_side_effects=True, vmem_limit_bytes=60 * MIB
        ),
        cost_estimate=pl.CostEstimate(
            flops=2 * tokens * depth * wide, bytes_accessed=4 * depth * wide + 4 * tokens * depth,
            transcendentals=0,
        ),
    )(hidden, residual, master)


def per_device(dp, tensor, hidden, residual, master, moment, second, gain, head, lengths, labels):
    gathered, stream = forward(dp, tensor, hidden, residual, master)
    w = gain * head
    a, b, loss = row_terms(stream, w, lengths, labels, w.shape[0] * dp)
    new_master, new_moment, new_second = update(
        gathered, stream, a, b, w[None, :], master, moment, second
    )
    return new_master, new_moment, new_second, loss


def solution(mesh):
    state = P("tensor", "dp")
    return jax.shard_map(
        functools.partial(per_device, mesh.shape["dp"], mesh.shape["tensor"]),
        mesh=mesh,
        in_specs=(P("dp", "tensor"), state, state, state, state, P("dp"), P("dp"), P(), P()),
        out_specs=(state, state, state, P()),
        check_vma=False,
    )
```

```python
import functools

import jax
import jax.numpy as jnp
from jax import lax
from jax.experimental import pallas as pl
from jax.experimental.pallas import tpu as pltpu
from jax.sharding import PartitionSpec as P

LEN = 128
STEP = 100
EPS_NORM = 1e-05
MIB = 1024 * 1024
MESH = pl.DeviceIdType.MESH


def update_kernel(ht_ref, s_ref, a_ref, b_ref, w_ref, p_ref, m_ref, v_ref, po_ref, mo_ref, vo_ref, cot):
    tile = p_ref.shape[0]

    @pl.when(pl.program_id(1) == 0)
    def _():
        a, b = a_ref[...].T, b_ref[...].T
        for seq in range(a.shape[1]):
            rows = slice(seq * LEN, (seq + 1) * LEN)
            value = a[:, seq : seq + 1] * w_ref[...] - b[:, seq : seq + 1] * s_ref[rows, :].astype(
                jnp.float32
            )
            cot[rows, :] = value.astype(jnp.bfloat16)

    start = pl.program_id(1) * tile
    part = 128

    def step(i, carry):
        rows = pl.ds(pl.multiple_of(i * part, part), part)
        at = pl.ds(pl.multiple_of(start + i * part, part), part)
        grad = jnp.dot(ht_ref[at, :], cot[...], preferred_element_type=jnp.float32)
        moment = 0.9 * m_ref[rows, :] + 0.1 * grad
        second = 0.95 * v_ref[rows, :] + 0.05 * grad * grad
        mo_ref[rows, :] = moment
        vo_ref[rows, :] = second
        m_hat = moment * (1.0 / (1.0 - 0.9**STEP))
        v_hat = second * (1.0 / (1.0 - 0.95**STEP))
        master = p_ref[rows, :]
        po_ref[rows, :] = master - 0.001 * (m_hat / (jnp.sqrt(v_hat) + 1e-08) + 0.1 * master)
        return carry

    for i in range(tile // part):
        step(i, 0)


def update(ht, stream, a, b, w, master, moment, second):
    ff, tokens = ht.shape
    wide = stream.shape[1]
    tile, cols = ff // 2, 256
    state = pl.BlockSpec((tile, cols), lambda j, i: (i, j))
    whole = lambda x: pl.BlockSpec(x.shape, lambda j, i: (0, 0), pipeline_mode=pl.Buffered(1))
    out = jax.ShapeDtypeStruct(master.shape, jnp.float32)
    return pl.pallas_call(
        update_kernel,
        grid=(wide // cols, ff // tile),
        in_specs=[
            whole(ht), pl.BlockSpec((tokens, cols), lambda j, i: (0, j)), whole(a), whole(b),
            pl.BlockSpec((1, cols), lambda j, i: (0, j)),
        ]
        + [state] * 3,
        out_specs=[state] * 3,
        out_shape=[out] * 3,
        scratch_shapes=[pltpu.VMEM((tokens, cols), jnp.bfloat16)],
        compiler_params=pltpu.CompilerParams(vmem_limit_bytes=48 * MIB),
        cost_estimate=pl.CostEstimate(
            flops=2 * tokens * ff * wide, bytes_accessed=24 * ff * wide, transcendentals=ff * wide
        ),
    )(ht, stream, a, b, w, master, moment, second)


def row_terms(squares, product, lengths, labels, full_width):
    lens = lengths.reshape(-1)
    lens_f = lens.astype(jnp.float32)[:, None]
    valid = jnp.arange(LEN, dtype=jnp.int32)[None, :] < lens[:, None]
    rstd = lax.rsqrt(squares / full_width + EPS_NORM)
    total = jnp.sum(jnp.where(valid, rstd * product, 0.0), 1)
    reward = (total / lens_f[:, 0]).reshape(-1, 2)
    chosen = jnp.where(labels == 1, reward[:, 1], reward[:, 0])
    other = jnp.where(labels == 1, reward[:, 0], reward[:, 1])
    margin = chosen - other
    loss = jnp.sum(jax.nn.softplus(-margin))
    sig = jax.nn.sigmoid(-margin)
    first = jnp.where(labels == 0, -sig, sig)
    dreward = jnp.stack([first, -first], 1).reshape(-1, 1)
    coef = jnp.where(valid, dreward / lens_f, 0.0)
    a = coef * rstd
    b = coef * (product * rstd**3 / full_width)
    return a, b, loss


def forward_kernel(dp, n, lanes, hidden, residual, w, master, hid_out, stream_out, sums_out, hid, hid_t,
                   stream, partial, sums, stage, weights, early_in, early_out, late_in, late_out, stage_sem, own_sem,
                   block_send, block_recv, ring_send, ring_recv, sums_send, sums_recv, out_sem):
    f32, bf16 = jnp.float32, jnp.bfloat16
    d, t = lax.axis_index("dp"), lax.axis_index("tensor")
    pairs = dp // 2
    q, core = d // 2, d % 2
    rows, wide = hidden.shape[0], master.shape[1]
    lane_cols, chunk = wide // lanes, rows // n
    mate = 2 * q + 1 - core

    def seat(place):
        place = lax.rem(place + n, n)
        return jnp.where(place < n // 2, 2 * place, 2 * (n - 1 - place) + 1)

    place = jnp.where(t % 2 == 0, t // 2, n - 1 - t // 2)
    right, left = seat(place + 1), seat(place - 1)

    def block(k):
        return 2 * lax.rem(q - k // 2 + pairs, pairs) + lax.rem(core + k, 2)

    def block_rows(k):
        return pl.ds(pl.multiple_of(block(k) * rows, rows), rows)

    depth = stage_rows(master.shape[0])
    pieces = master.shape[0] // depth

    def stage_copy(i):
        at = pl.ds(pl.multiple_of(i * depth, depth), depth)
        return pltpu.make_async_copy(master.at[at], stage.at[at], stage_sem.at[i])

    for i in range(pieces):
        stage_copy(i).start()
    own_copy = pltpu.make_async_copy(hidden, hid.at[block_rows(0)], own_sem)
    own_copy.start()

    barrier = pltpu.get_barrier_semaphore()
    greeted = [{"tensor": right}, {"tensor": left}]
    greeted += [{"dp": lax.rem(d + j, dp)} for j in range(1, dp)]
    for other in greeted:
        pl.semaphore_signal(barrier, inc=1, device_id=other, device_id_type=MESH)
    pl.semaphore_wait(barrier, len(greeted))

    def block_copy(k):
        if k == 1 or k % 2 == 0:
            src, at = hidden, block_rows(0)
        else:
            src, at = hid.at[block_rows(k - 1)], block_rows(k - 1)
        to = mate if k % 2 else 2 * lax.rem(q + k // 2, pairs) + core
        return pltpu.make_async_remote_copy(
            src_ref=src, dst_ref=hid.at[at], send_sem=block_send.at[k - 1], recv_sem=block_recv.at[k - 1],
            device_id={"dp": to}, device_id_type=MESH,
        )

    def block_wait(k):
        pltpu.make_async_remote_copy(
            src_ref=hidden, dst_ref=hid.at[block_rows(k)], send_sem=block_send.at[k - 1],
            recv_sem=block_recv.at[k - 1], device_id={"dp": mate}, device_id_type=MESH,
        ).wait_recv()

    for k in [1] + list(range(2, dp, 2)):
        block_copy(k).start()

    def to_weights(i, carry):
        stage_copy(i).wait()
        at = pl.ds(pl.multiple_of(i * depth, depth), depth)
        weights[at, :] = stage[at, :].astype(bf16)
        return carry

    lax.fori_loop(0, pieces, to_weights, 0)

    def multiply(k):
        at = block_rows(k)

        def tile(c, carry):
            cols = pl.ds(pl.multiple_of(c * 256, 256), 256)
            partial[k, :, cols] = jnp.dot(hid[at, :], weights[:, cols], preferred_element_type=f32)
            return carry

        lax.fori_loop(0, wide // 256, tile, 0)
        res_rows = residual.shape[0]

        @pl.when(block(k) == t * res_rows // rows)
        def _():
            own = pl.ds(pl.multiple_of(lax.rem(t * res_rows, rows), res_rows), res_rows)
            partial[k, own, :] += residual[...].astype(f32)

    sets = [(0, 0, 2, early_in, early_out), (1, 2, dp - 2, late_in, late_out)]

    def chunk_at(lane, offset):
        mirrored = place if lane % 2 == 0 else n - place
        index = lax.rem(mirrored + offset + 2 * n, n)
        return pl.ds(pl.multiple_of(index * chunk, chunk), chunk)

    def ring_copy(which, lane, step, src, dst):
        return pltpu.make_async_remote_copy(
            src_ref=src, dst_ref=dst, send_sem=ring_send.at[which, lane, step],
            recv_sem=ring_recv.at[which, lane, step],
            device_id={"tensor": right if lane % 2 == 0 else left}, device_id_type=MESH,
        )

    def sum_copy(group, lane, step):
        which, first, count, arrive, leave = group
        return ring_copy(which, lane, step, leave.at[lane, step], arrive.at[lane, step])

    def share_copy(group, lane, step, offset):
        which, first, count, arrive, leave = group
        at = stream.at[pl.ds(first, count), chunk_at(lane, offset), pl.ds(lane * lane_cols, lane_cols)]
        return ring_copy(which, lane, n - 1 + step, at, at)

    def own_part(group, lane, offset):
        which, first, count, arrive, leave = group
        return partial[pl.ds(first, count), chunk_at(lane, offset), pl.ds(lane * lane_cols, lane_cols)]

    def begin(group):
        for lane in range(lanes):
            group[4][lane, 0] = own_part(group, lane, 0).astype(bf16)
            sum_copy(group, lane, 0).start()

    def add_step(group, step):
        for lane in range(lanes):
            sum_copy(group, lane, step - 1).wait_recv()
            total = group[3][lane, step - 1].astype(f32) + own_part(group, lane, -step)
            group[4][lane, step] = total.astype(bf16)
            sum_copy(group, lane, step).start()

    def turn(group):
        which, first, count, arrive, leave = group
        for lane in range(lanes):
            sum_copy(group, lane, n - 2).wait_recv()
            total = arrive[lane, n - 2].astype(f32) + own_part(group, lane, 1)
            cols = pl.ds(lane * lane_cols, lane_cols)
            stream[pl.ds(first, count), chunk_at(lane, 1), cols] = total.astype(bf16)
            share_copy(group, lane, 0, 1).start()

    def share_step(group, step):
        for lane in range(lanes):
            share_copy(group, lane, step - 1, 1 - step).wait_recv()
            share_copy(group, lane, step, 1 - step).start()

    def finish(group):
        for lane in range(lanes):
            share_copy(group, lane, n - 2, 2 - n).wait_recv()

    def sent(group):
        for lane in range(lanes):

            def wait(step, carry):
                sum_copy(group, lane, step).wait_send()
                share_copy(group, lane, step, 1 - step).wait_send()
                return carry

            lax.fori_loop(0, n - 1, wait, 0)

    def result_copy(k):
        return pltpu.make_async_copy(stream.at[k], stream_out.at[block_rows(k)], out_sem.at[k])

    def block_sums(k):
        for seq in range(rows // LEN):
            at = slice(seq * LEN, (seq + 1) * LEN)
            squares = jnp.zeros((LEN, 128), f32)
            product = jnp.zeros((LEN, 128), f32)
            for c in range(wide // 128):
                cols = slice(c * 128, (c + 1) * 128)
                value = stream[k, at, cols].astype(f32)
                squares += value * value
                product += value * w[:, cols]
            sums[d, block(k), 0, seq : seq + 1, :] = jnp.sum(squares.T, 0, keepdims=True)
            sums[d, block(k), 1, seq : seq + 1, :] = jnp.sum(product.T, 0, keepdims=True)

    def sums_copy(j, source):
        return pltpu.make_async_remote_copy(
            src_ref=sums.at[d], dst_ref=sums.at[source], send_sem=sums_send.at[j - 1],
            recv_sem=sums_recv.at[j - 1], device_id={"dp": lax.rem(d + j, dp)}, device_id_type=MESH,
        )

    units = hid.shape[1] // 128
    per_step = -(-units // (n - 2))

    def turn_unit(i):
        @pl.when(i < units)
        def _():
            cols = pl.ds(pl.multiple_of(i * 128, 128), 128)
            hid_t[cols, :] = hid[:, cols].T

    early, late = sets
    own_copy.wait()
    multiply(0)
    block_wait(1)
    multiply(1)
    begin(early)

    def early_sums(step, carry):
        add_step(early, step)
        return carry

    lax.fori_loop(1, n - 1, early_sums, 0)
    turn(early)
    for k in range(2, dp, 2):
        block_wait(k)
        block_copy(k + 1).start()
    for k in range(2, dp):
        if k % 2:
            block_wait(k)
        multiply(k)
    hid_copy = pltpu.make_async_copy(hid_t, hid_out, out_sem.at[dp])
    begin(late)

    def both(step, carry):
        share_step(early, step)
        add_step(late, step)
        for j in range(per_step):
            turn_unit((step - 1) * per_step + j)
        return carry

    lax.fori_loop(1, n - 1, both, 0)
    finish(early)
    turn(late)
    hid_copy.start()
    for k in range(2):
        result_copy(k).start()
        block_sums(k)

    def late_shares(step, carry):
        share_step(late, step)
        return carry

    lax.fori_loop(1, n - 1, late_shares, 0)
    finish(late)
    for k in range(2, dp):
        result_copy(k).start()
        block_sums(k)
    for j in range(1, dp):
        sums_copy(j, d).start()
    for k in range(1, dp):
        block_copy(k).wait_send()
    sent(early)
    sent(late)
    for j in range(1, dp):
        sums_copy(j, lax.rem(d - j + dp, dp)).wait_recv()
    total = sums[0]
    for source in range(1, dp):
        total += sums[source]
    sums_out[...] = total
    for j in range(1, dp):
        sums_copy(j, d).wait_send()
    for k in range(dp):
        result_copy(k).wait()
    hid_copy.wait()


def stage_rows(depth):
    return 128 if depth % 128 == 0 else depth


def forward(dp, n, hidden, residual, w, master):
    rows, depth = hidden.shape
    wide = master.shape[1]
    tokens = rows * dp
    lanes = 4
    chunk, lane_cols = rows // n, wide // lanes
    bf16 = jnp.bfloat16
    slots = lambda count: pltpu.VMEM((lanes, n - 1, count, chunk, lane_cols), bf16)
    dma = pltpu.SemaphoreType.DMA
    vmem = pl.BlockSpec(memory_space=pltpu.VMEM)
    hbm = pl.BlockSpec(memory_space=pl.ANY)
    return pl.pallas_call(
        functools.partial(forward_kernel, dp, n, lanes),
        in_specs=[vmem, vmem, vmem, hbm],
        out_specs=[hbm, hbm, vmem],
        out_shape=[
            jax.ShapeDtypeStruct((depth, tokens), bf16),
            jax.ShapeDtypeStruct((tokens, wide), bf16),
            jax.ShapeDtypeStruct((dp, 2, rows // LEN, LEN), jnp.float32),
        ],
        scratch_shapes=[
            pltpu.VMEM((tokens, depth), bf16),
            pltpu.VMEM((depth, tokens), bf16),
            pltpu.VMEM((dp, rows, wide), bf16),
            pltpu.VMEM((dp, rows, wide), jnp.float32),
            pltpu.VMEM((dp, dp, 2, rows // LEN, LEN), jnp.float32),
            pltpu.VMEM((depth, wide), jnp.float32),
            pltpu.VMEM((depth, wide), bf16),
            slots(2), slots(2), slots(dp - 2), slots(dp - 2),
            dma((depth // stage_rows(depth),)),
            dma,
            dma((dp - 1,)), dma((dp - 1,)),
            dma((2, lanes, 2 * n - 2)), dma((2, lanes, 2 * n - 2)),
            dma((dp - 1,)), dma((dp - 1,)),
            dma((dp + 1,)),
        ],
        compiler_params=pltpu.CompilerParams(
            collective_id=0, has_side_effects=True, vmem_limit_bytes=60 * MIB
        ),
        cost_estimate=pl.CostEstimate(
            flops=2 * tokens * depth * wide, bytes_accessed=4 * depth * wide + 4 * tokens * depth,
            transcendentals=0,
        ),
    )(hidden, residual, w, master)


def per_device(dp, tensor, hidden, residual, master, moment, second, gain, head, lengths, labels):
    w = (gain * head)[None, :]
    hidden_t, stream, sums = forward(dp, tensor, hidden, residual, w, master)
    squares, product = sums[:, 0].reshape(-1, LEN), sums[:, 1].reshape(-1, LEN)
    a, b, loss = row_terms(squares, product, lengths, labels, w.shape[1] * dp)
    new_master, new_moment, new_second = update(
        hidden_t, stream, a, b, w, master, moment, second
    )
    return new_master, new_moment, new_second, loss


def solution(mesh):
    state = P("tensor", "dp")
    return jax.shard_map(
        functools.partial(per_device, mesh.shape["dp"], mesh.shape["tensor"]),
        mesh=mesh,
        in_specs=(P("dp", "tensor"), state, state, state, state, P("dp"), P("dp"), P(), P()),
        out_specs=(state, state, state, P()),
        check_vma=False,
    )
```

```python
import functools

import jax
import jax.numpy as jnp
from jax import lax
from jax.experimental import pallas as pl
from jax.experimental.pallas import tpu as pltpu
from jax.sharding import PartitionSpec as P

LEN = 128
STEP = 100
EPS_NORM = 1e-05
MIB = 1024 * 1024
MESH = pl.DeviceIdType.MESH


def update_kernel(ht_ref, s_ref, a_ref, b_ref, w_ref, p_ref, m_ref, v_ref, po_ref, mo_ref, vo_ref, cot):
    tile = p_ref.shape[0]

    @pl.when(pl.program_id(1) == 0)
    def _():
        a, b = a_ref[...].T, b_ref[...].T
        for seq in range(a.shape[1]):
            rows = slice(seq * LEN, (seq + 1) * LEN)
            value = a[:, seq : seq + 1] * w_ref[...] - b[:, seq : seq + 1] * s_ref[rows, :].astype(
                jnp.float32
            )
            cot[rows, :] = value.astype(jnp.bfloat16)

    start = pl.program_id(1) * tile
    part = 128

    def step(i, carry):
        rows = pl.ds(pl.multiple_of(i * part, part), part)
        at = pl.ds(pl.multiple_of(start + i * part, part), part)
        grad = jnp.dot(ht_ref[at, :], cot[...], preferred_element_type=jnp.float32)
        moment = 0.9 * m_ref[rows, :] + 0.1 * grad
        second = 0.95 * v_ref[rows, :] + 0.05 * grad * grad
        mo_ref[rows, :] = moment
        vo_ref[rows, :] = second
        m_hat = moment * (1.0 / (1.0 - 0.9**STEP))
        v_hat = second * (1.0 / (1.0 - 0.95**STEP))
        master = p_ref[rows, :]
        po_ref[rows, :] = master - 0.001 * (m_hat / (jnp.sqrt(v_hat) + 1e-08) + 0.1 * master)
        return carry

    for i in range(tile // part):
        step(i, 0)


def update(ht, stream, a, b, w, master, moment, second):
    ff, tokens = ht.shape
    wide = stream.shape[1]
    tile, cols = ff // 2, 256
    state = pl.BlockSpec((tile, cols), lambda j, i: (i, j))
    whole = lambda x: pl.BlockSpec(x.shape, lambda j, i: (0, 0), pipeline_mode=pl.Buffered(1))
    out = jax.ShapeDtypeStruct(master.shape, jnp.float32)
    return pl.pallas_call(
        update_kernel,
        grid=(wide // cols, ff // tile),
        in_specs=[
            whole(ht), pl.BlockSpec((tokens, cols), lambda j, i: (0, j)), whole(a), whole(b),
            pl.BlockSpec((1, cols), lambda j, i: (0, j)),
        ]
        + [state] * 3,
        out_specs=[state] * 3,
        out_shape=[out] * 3,
        scratch_shapes=[pltpu.VMEM((tokens, cols), jnp.bfloat16)],
        compiler_params=pltpu.CompilerParams(vmem_limit_bytes=20 * MIB),
        cost_estimate=pl.CostEstimate(
            flops=2 * tokens * ff * wide, bytes_accessed=24 * ff * wide, transcendentals=ff * wide
        ),
    )(ht, stream, a, b, w, master, moment, second)


def row_terms(squares, product, lengths, labels, full_width):
    lens = lengths.reshape(-1)
    lens_f = lens.astype(jnp.float32)[:, None]
    valid = jnp.arange(LEN, dtype=jnp.int32)[None, :] < lens[:, None]
    rstd = lax.rsqrt(squares / full_width + EPS_NORM)
    total = jnp.sum(jnp.where(valid, rstd * product, 0.0), 1)
    reward = (total / lens_f[:, 0]).reshape(-1, 2)
    chosen = jnp.where(labels == 1, reward[:, 1], reward[:, 0])
    other = jnp.where(labels == 1, reward[:, 0], reward[:, 1])
    margin = chosen - other
    loss = jnp.sum(jax.nn.softplus(-margin))
    sig = jax.nn.sigmoid(-margin)
    first = jnp.where(labels == 0, -sig, sig)
    dreward = jnp.stack([first, -first], 1).reshape(-1, 1)
    coef = jnp.where(valid, dreward / lens_f, 0.0)
    a = coef * rstd
    b = coef * (product * rstd**3 / full_width)
    return a, b, loss


def forward_kernel(dp, n, lanes, hidden, residual, w, master, hid_out, stream_out, sums_out, hid, hid_t,
                   stream, partial, sums, stage, weights, early_in, early_out, late_in, late_out, stage_sem, own_sem,
                   block_send, block_recv, ring_send, ring_recv, sums_send, sums_recv, out_sem):
    f32, bf16 = jnp.float32, jnp.bfloat16
    d, t = lax.axis_index("dp"), lax.axis_index("tensor")
    pairs = dp // 2
    q, core = d // 2, d % 2
    rows, wide = hidden.shape[0], master.shape[1]
    lane_cols, chunk = wide // lanes, rows // n
    mate = 2 * q + 1 - core

    def seat(place):
        place = lax.rem(place + n, n)
        return jnp.where(place < n // 2, 2 * place, 2 * (n - 1 - place) + 1)

    place = jnp.where(t % 2 == 0, t // 2, n - 1 - t // 2)
    right, left = seat(place + 1), seat(place - 1)

    def block(k):
        return 2 * lax.rem(q - k // 2 + pairs, pairs) + lax.rem(core + k, 2)

    def block_rows(k):
        return pl.ds(pl.multiple_of(block(k) * rows, rows), rows)

    depth = stage_rows(master.shape[0])
    pieces = master.shape[0] // depth

    def stage_copy(i):
        at = pl.ds(pl.multiple_of(i * depth, depth), depth)
        slot = lax.rem(i, slots)
        return pltpu.make_async_copy(master.at[at], stage.at[slot], stage_sem.at[slot])

    slots = stage.shape[0]
    for i in range(slots):
        stage_copy(i).start()
    own_copy = pltpu.make_async_copy(hidden, hid.at[block_rows(0)], own_sem)
    own_copy.start()

    barrier = pltpu.get_barrier_semaphore()
    greeted = [{"tensor": right}, {"tensor": left}]
    greeted += [{"dp": lax.rem(d + j, dp)} for j in range(1, dp)]
    for other in greeted:
        pl.semaphore_signal(barrier, inc=1, device_id=other, device_id_type=MESH)
    pl.semaphore_wait(barrier, len(greeted))

    def block_copy(k):
        if k == 1 or k % 2 == 0:
            src, at = hidden, block_rows(0)
        else:
            src, at = hid.at[block_rows(k - 1)], block_rows(k - 1)
        to = mate if k % 2 else 2 * lax.rem(q + k // 2, pairs) + core
        return pltpu.make_async_remote_copy(
            src_ref=src, dst_ref=hid.at[at], send_sem=block_send.at[k - 1], recv_sem=block_recv.at[k - 1],
            device_id={"dp": to}, device_id_type=MESH,
        )

    def block_wait(k):
        pltpu.make_async_remote_copy(
            src_ref=hidden, dst_ref=hid.at[block_rows(k)], send_sem=block_send.at[k - 1],
            recv_sem=block_recv.at[k - 1], device_id={"dp": mate}, device_id_type=MESH,
        ).wait_recv()

    for k in [1] + list(range(2, dp, 2)):
        block_copy(k).start()

    def to_weights(i, carry):
        stage_copy(i).wait()
        at = pl.ds(pl.multiple_of(i * depth, depth), depth)
        weights[at, :] = stage[lax.rem(i, slots)].astype(bf16)

        @pl.when(i + slots < pieces)
        def _():
            stage_copy(i + slots).start()

        return carry

    lax.fori_loop(0, pieces, to_weights, 0)

    tiles = wide // 256

    def multiply_tile(k, c):
        cols = pl.ds(pl.multiple_of(c * 256, 256), 256)
        partial[k, :, cols] = jnp.dot(
            hid[block_rows(k), :], weights[:, cols], preferred_element_type=f32
        ).astype(bf16)

    def add_residual(k):
        res_rows = residual.shape[0]

        @pl.when(block(k) == t * res_rows // rows)
        def _():
            own = pl.ds(pl.multiple_of(lax.rem(t * res_rows, rows), res_rows), res_rows)
            total = partial[k, own, :].astype(f32) + residual[...].astype(f32)
            partial[k, own, :] = total.astype(bf16)

    def multiply(k):
        def tile(c, carry):
            multiply_tile(k, c)
            return carry

        lax.fori_loop(0, tiles, tile, 0)
        add_residual(k)

    sets = [(0, 0, 2, early_in, early_out), (1, 2, dp - 2, late_in, late_out)]

    def chunk_at(lane, offset):
        mirrored = place if lane % 2 == 0 else n - place
        index = lax.rem(mirrored + offset + 2 * n, n)
        return pl.ds(pl.multiple_of(index * chunk, chunk), chunk)

    def ring_copy(which, lane, step, src, dst):
        return pltpu.make_async_remote_copy(
            src_ref=src, dst_ref=dst, send_sem=ring_send.at[which, lane, step],
            recv_sem=ring_recv.at[which, lane, step],
            device_id={"tensor": right if lane % 2 == 0 else left}, device_id_type=MESH,
        )

    def sum_copy(group, lane, step):
        which, first, count, arrive, leave = group
        src = leave.at[lane] if step is None else arrive.at[lane, step - 1]
        at = 0 if step is None else step
        return ring_copy(which, lane, at, src, arrive.at[lane, at])

    def arrival(group, lane, step):
        which, first, count, arrive, leave = group
        return ring_copy(which, lane, step, leave.at[lane], arrive.at[lane, step])

    def share_copy(group, lane, step, offset):
        which, first, count, arrive, leave = group
        at = stream.at[pl.ds(first, count), chunk_at(lane, offset), pl.ds(lane * lane_cols, lane_cols)]
        return ring_copy(which, lane, n - 1 + step, at, at)

    def own_part(group, lane, offset):
        which, first, count, arrive, leave = group
        return partial[pl.ds(first, count), chunk_at(lane, offset), pl.ds(lane * lane_cols, lane_cols)]

    def begin(group):
        for lane in range(lanes):
            group[4][lane] = own_part(group, lane, 0)
            sum_copy(group, lane, None).start()

    def add_step(group, step):
        for lane in range(lanes):
            arrival(group, lane, step - 1).wait_recv()
            total = group[3][lane, step - 1].astype(f32) + own_part(group, lane, -step).astype(f32)
            group[3][lane, step - 1] = total.astype(bf16)
            sum_copy(group, lane, step).start()

    def turn(group):
        which, first, count, arrive, leave = group
        for lane in range(lanes):
            arrival(group, lane, n - 2).wait_recv()
            total = arrive[lane, n - 2].astype(f32) + own_part(group, lane, 1).astype(f32)
            cols = pl.ds(lane * lane_cols, lane_cols)
            stream[pl.ds(first, count), chunk_at(lane, 1), cols] = total.astype(bf16)
            share_copy(group, lane, 0, 1).start()

    def share_step(group, step):
        for lane in range(lanes):
            share_copy(group, lane, step - 1, 1 - step).wait_recv()
            share_copy(group, lane, step, 1 - step).start()

    def finish(group):
        for lane in range(lanes):
            share_copy(group, lane, n - 2, 2 - n).wait_recv()

    def sent(group):
        for lane in range(lanes):

            def wait(step, carry):
                arrival(group, lane, step).wait_send()
                share_copy(group, lane, step, 1 - step).wait_send()
                return carry

            lax.fori_loop(0, n - 1, wait, 0)

    def result_copy(k):
        return pltpu.make_async_copy(stream.at[k], stream_out.at[block_rows(k)], out_sem.at[k])

    def block_sums(k):
        for seq in range(rows // LEN):
            at = slice(seq * LEN, (seq + 1) * LEN)
            squares = jnp.zeros((LEN, 128), f32)
            product = jnp.zeros((LEN, 128), f32)
            for c in range(wide // 128):
                cols = slice(c * 128, (c + 1) * 128)
                value = stream[k, at, cols].astype(f32)
                squares += value * value
                product += value * w[:, cols]
            sums[d, block(k), 0, seq : seq + 1, :] = jnp.sum(squares.T, 0, keepdims=True)
            sums[d, block(k), 1, seq : seq + 1, :] = jnp.sum(product.T, 0, keepdims=True)

    def sums_copy(j, source):
        return pltpu.make_async_remote_copy(
            src_ref=sums.at[d], dst_ref=sums.at[source], send_sem=sums_send.at[j - 1],
            recv_sem=sums_recv.at[j - 1], device_id={"dp": lax.rem(d + j, dp)}, device_id_type=MESH,
        )

    units = hid.shape[1] // 128
    per_step = -(-units // (n - 2))

    def turn_unit(i):
        @pl.when(i < units)
        def _():
            cols = pl.ds(pl.multiple_of(i * 128, 128), 128)
            hid_t[cols, :] = hid[:, cols].T

    early, late = sets
    own_copy.wait()
    multiply(0)
    block_wait(1)
    multiply(1)
    begin(early)

    def early_sums(step, carry):
        add_step(early, step)
        return carry

    def early_sums_and_tiles(step, carry):
        add_step(early, step)

        def tile(j, inner):
            i = (step - middle) * tiles_per_step + j

            @pl.when(i < late_tiles)
            def _():
                multiply_tile(2 + i // tiles, lax.rem(i, tiles))

            return inner

        lax.fori_loop(0, tiles_per_step, tile, 0)
        return carry

    first, middle = (n - 1) // 3, (n - 1) // 3 + 2
    late_tiles = (dp - 2) * tiles
    tiles_per_step = -(-late_tiles // (n - 1 - middle))
    lax.fori_loop(1, first + 1, early_sums, 0)
    for k in range(2, dp, 2):
        block_wait(k)
        block_copy(k + 1).start()
    lax.fori_loop(first + 1, middle, early_sums, 0)
    for k in range(3, dp, 2):
        block_wait(k)
    lax.fori_loop(middle, n - 1, early_sums_and_tiles, 0)
    turn(early)
    for k in range(2, dp):
        add_residual(k)
    hid_copy = pltpu.make_async_copy(hid_t, hid_out, out_sem.at[dp])
    begin(late)

    def both(step, carry):
        share_step(early, step)
        add_step(late, step)
        for j in range(per_step):
            turn_unit((step - 1) * per_step + j)
        return carry

    lax.fori_loop(1, n - 1, both, 0)
    finish(early)
    turn(late)
    hid_copy.start()
    for k in range(2):
        result_copy(k).start()
        block_sums(k)

    def late_shares(step, carry):
        share_step(late, step)
        return carry

    lax.fori_loop(1, n - 1, late_shares, 0)
    finish(late)
    for k in range(2, dp):
        result_copy(k).start()
        block_sums(k)
    for j in range(1, dp):
        sums_copy(j, d).start()
    for k in range(1, dp):
        block_copy(k).wait_send()
    sent(early)
    sent(late)
    for j in range(1, dp):
        sums_copy(j, lax.rem(d - j + dp, dp)).wait_recv()
    total = sums[0]
    for source in range(1, dp):
        total += sums[source]
    sums_out[...] = total
    for j in range(1, dp):
        sums_copy(j, d).wait_send()
    for k in range(dp):
        result_copy(k).wait()
    hid_copy.wait()


def stage_rows(depth):
    return 128 if depth % 128 == 0 else depth


def forward(dp, n, hidden, residual, w, master):
    rows, depth = hidden.shape
    wide = master.shape[1]
    tokens = rows * dp
    lanes = 4
    chunk, lane_cols = rows // n, wide // lanes
    bf16 = jnp.bfloat16
    slots = lambda count: pltpu.VMEM((lanes, n - 1, count, chunk, lane_cols), bf16)
    first_slot = lambda count: pltpu.VMEM((lanes, count, chunk, lane_cols), bf16)
    dma = pltpu.SemaphoreType.DMA
    vmem = pl.BlockSpec(memory_space=pltpu.VMEM)
    hbm = pl.BlockSpec(memory_space=pl.ANY)
    return pl.pallas_call(
        functools.partial(forward_kernel, dp, n, lanes),
        in_specs=[vmem, vmem, vmem, hbm],
        out_specs=[hbm, hbm, vmem],
        out_shape=[
            jax.ShapeDtypeStruct((depth, tokens), bf16),
            jax.ShapeDtypeStruct((tokens, wide), bf16),
            jax.ShapeDtypeStruct((dp, 2, rows // LEN, LEN), jnp.float32),
        ],
        scratch_shapes=[
            pltpu.VMEM((tokens, depth), bf16),
            pltpu.VMEM((depth, tokens), bf16),
            pltpu.VMEM((dp, rows, wide), bf16),
            pltpu.VMEM((dp, rows, wide), bf16),
            pltpu.VMEM((dp, dp, 2, rows // LEN, LEN), jnp.float32),
            pltpu.VMEM((3, stage_rows(depth), wide), jnp.float32),
            pltpu.VMEM((depth, wide), bf16),
            slots(2), first_slot(2), slots(dp - 2), first_slot(dp - 2),
            dma((3,)),
            dma,
            dma((dp - 1,)), dma((dp - 1,)),
            dma((2, lanes, 2 * n - 2)), dma((2, lanes, 2 * n - 2)),
            dma((dp - 1,)), dma((dp - 1,)),
            dma((dp + 1,)),
        ],
        compiler_params=pltpu.CompilerParams(
            collective_id=0, has_side_effects=True, vmem_limit_bytes=34 * MIB
        ),
        cost_estimate=pl.CostEstimate(
            flops=2 * tokens * depth * wide, bytes_accessed=4 * depth * wide + 4 * tokens * depth,
            transcendentals=0,
        ),
    )(hidden, residual, w, master)


def per_device(dp, tensor, hidden, residual, master, moment, second, gain, head, lengths, labels):
    w = (gain * head)[None, :]
    hidden_t, stream, sums = forward(dp, tensor, hidden, residual, w, master)
    squares, product = sums[:, 0].reshape(-1, LEN), sums[:, 1].reshape(-1, LEN)
    a, b, loss = row_terms(squares, product, lengths, labels, w.shape[1] * dp)
    new_master, new_moment, new_second = update(
        hidden_t, stream, a, b, w, master, moment, second
    )
    return new_master, new_moment, new_second, loss


def solution(mesh):
    state = P("tensor", "dp")
    return jax.shard_map(
        functools.partial(per_device, mesh.shape["dp"], mesh.shape["tensor"]),
        mesh=mesh,
        in_specs=(P("dp", "tensor"), state, state, state, state, P("dp"), P("dp"), P(), P()),
        out_specs=(state, state, state, P()),
        check_vma=False,
    )
```

```python
import functools

import jax
import jax.numpy as jnp
from jax import lax
from jax.experimental import pallas as pl
from jax.experimental.pallas import tpu as pltpu
from jax.sharding import PartitionSpec as P

LEN = 128
STEP = 100
EPS_NORM = 1e-05
MIB = 1024 * 1024
MESH = pl.DeviceIdType.MESH


def update_kernel(ht_ref, s_ref, a_ref, b_ref, w_ref, p_ref, m_ref, v_ref, po_ref, mo_ref, vo_ref, cot):
    tile = p_ref.shape[0]

    @pl.when(pl.program_id(1) == 0)
    def _():
        a, b = a_ref[...].T, b_ref[...].T
        for seq in range(a.shape[1]):
            rows = slice(seq * LEN, (seq + 1) * LEN)
            value = a[:, seq : seq + 1] * w_ref[...] - b[:, seq : seq + 1] * s_ref[rows, :].astype(
                jnp.float32
            )
            cot[rows, :] = value.astype(jnp.bfloat16)

    start = pl.program_id(1) * tile
    part = 128

    def step(i, carry):
        rows = pl.ds(pl.multiple_of(i * part, part), part)
        at = pl.ds(pl.multiple_of(start + i * part, part), part)
        grad = jnp.dot(ht_ref[at, :], cot[...], preferred_element_type=jnp.float32)
        moment = 0.9 * m_ref[rows, :] + 0.1 * grad
        second = 0.95 * v_ref[rows, :] + 0.05 * grad * grad
        mo_ref[rows, :] = moment
        vo_ref[rows, :] = second
        m_hat = moment * (1.0 / (1.0 - 0.9**STEP))
        v_hat = second * (1.0 / (1.0 - 0.95**STEP))
        master = p_ref[rows, :]
        po_ref[rows, :] = master - 0.001 * (m_hat / (jnp.sqrt(v_hat) + 1e-08) + 0.1 * master)
        return carry

    for i in range(tile // part):
        step(i, 0)


def update(ht, stream, a, b, w, master, moment, second):
    ff, tokens = ht.shape
    wide = stream.shape[1]
    tile, cols = ff // 2, 256
    state = pl.BlockSpec((tile, cols), lambda j, i: (i, j))
    whole = lambda x: pl.BlockSpec(x.shape, lambda j, i: (0, 0), pipeline_mode=pl.Buffered(1))
    out = jax.ShapeDtypeStruct(master.shape, jnp.float32)
    return pl.pallas_call(
        update_kernel,
        grid=(wide // cols, ff // tile),
        in_specs=[
            whole(ht), pl.BlockSpec((tokens, cols), lambda j, i: (0, j)), whole(a), whole(b),
            pl.BlockSpec((1, cols), lambda j, i: (0, j)),
        ]
        + [state] * 3,
        out_specs=[state] * 3,
        out_shape=[out] * 3,
        scratch_shapes=[pltpu.VMEM((tokens, cols), jnp.bfloat16)],
        compiler_params=pltpu.CompilerParams(vmem_limit_bytes=48 * MIB),
        cost_estimate=pl.CostEstimate(
            flops=2 * tokens * ff * wide, bytes_accessed=24 * ff * wide, transcendentals=ff * wide
        ),
    )(ht, stream, a, b, w, master, moment, second)


def row_terms(squares, product, lengths, labels, full_width):
    lens = lengths.reshape(-1)
    lens_f = lens.astype(jnp.float32)[:, None]
    valid = jnp.arange(LEN, dtype=jnp.int32)[None, :] < lens[:, None]
    rstd = lax.rsqrt(squares / full_width + EPS_NORM)
    total = jnp.sum(jnp.where(valid, rstd * product, 0.0), 1)
    reward = (total / lens_f[:, 0]).reshape(-1, 2)
    chosen = jnp.where(labels == 1, reward[:, 1], reward[:, 0])
    other = jnp.where(labels == 1, reward[:, 0], reward[:, 1])
    margin = chosen - other
    loss = jnp.sum(jax.nn.softplus(-margin))
    sig = jax.nn.sigmoid(-margin)
    first = jnp.where(labels == 0, -sig, sig)
    dreward = jnp.stack([first, -first], 1).reshape(-1, 1)
    coef = jnp.where(valid, dreward / lens_f, 0.0)
    a = coef * rstd
    b = coef * (product * rstd**3 / full_width)
    return a, b, loss


def forward_kernel(dp, n, lanes, hidden, residual, w, master, hid_out, stream_out, sums_out, hid, hid_t,
                   stream, partial, sums, stage, weights, early_in, early_out, late_in, late_out, stage_sem, own_sem,
                   block_send, block_recv, ring_send, ring_recv, sums_send, sums_recv, out_sem):
    f32, bf16 = jnp.float32, jnp.bfloat16
    d, t = lax.axis_index("dp"), lax.axis_index("tensor")
    pairs = dp // 2
    q, core = d // 2, d % 2
    rows, wide = hidden.shape[0], master.shape[1]
    lane_cols, chunk = wide // lanes, rows // n
    mate = 2 * q + 1 - core

    def seat(place):
        place = lax.rem(place + n, n)
        return jnp.where(place < n // 2, 2 * place, 2 * (n - 1 - place) + 1)

    place = jnp.where(t % 2 == 0, t // 2, n - 1 - t // 2)
    right, left = seat(place + 1), seat(place - 1)

    def block(k):
        return 2 * lax.rem(q - k // 2 + pairs, pairs) + lax.rem(core + k, 2)

    def block_rows(k):
        return pl.ds(pl.multiple_of(block(k) * rows, rows), rows)

    depth = stage_rows(master.shape[0])
    pieces = master.shape[0] // depth

    def stage_copy(i):
        at = pl.ds(pl.multiple_of(i * depth, depth), depth)
        slot = lax.rem(i, slots)
        return pltpu.make_async_copy(master.at[at], stage.at[slot], stage_sem.at[slot])

    slots = stage.shape[0]
    for i in range(slots):
        stage_copy(i).start()
    own_copy = pltpu.make_async_copy(hidden, hid.at[block_rows(0)], own_sem)
    own_copy.start()

    barrier = pltpu.get_barrier_semaphore()
    greeted = [{"tensor": right}, {"tensor": left}]
    greeted += [{"dp": lax.rem(d + j, dp)} for j in range(1, dp)]
    for other in greeted:
        pl.semaphore_signal(barrier, inc=1, device_id=other, device_id_type=MESH)
    pl.semaphore_wait(barrier, len(greeted))

    def block_copy(k):
        if k == 1 or k % 2 == 0:
            src, at = hidden, block_rows(0)
        else:
            src, at = hid.at[block_rows(k - 1)], block_rows(k - 1)
        to = mate if k % 2 else 2 * lax.rem(q + k // 2, pairs) + core
        return pltpu.make_async_remote_copy(
            src_ref=src, dst_ref=hid.at[at], send_sem=block_send.at[k - 1], recv_sem=block_recv.at[k - 1],
            device_id={"dp": to}, device_id_type=MESH,
        )

    def block_wait(k):
        pltpu.make_async_remote_copy(
            src_ref=hidden, dst_ref=hid.at[block_rows(k)], send_sem=block_send.at[k - 1],
            recv_sem=block_recv.at[k - 1], device_id={"dp": mate}, device_id_type=MESH,
        ).wait_recv()

    for k in [1] + list(range(2, dp, 2)):
        block_copy(k).start()

    def to_weights(i, carry):
        stage_copy(i).wait()
        at = pl.ds(pl.multiple_of(i * depth, depth), depth)
        weights[at, :] = stage[lax.rem(i, slots)].astype(bf16)

        @pl.when(i + slots < pieces)
        def _():
            stage_copy(i + slots).start()

        return carry

    lax.fori_loop(0, pieces, to_weights, 0)

    tiles = wide // 256

    def multiply_tile(k, c):
        cols = pl.ds(pl.multiple_of(c * 256, 256), 256)
        partial[k, :, cols] = jnp.dot(
            hid[block_rows(k), :], weights[:, cols], preferred_element_type=f32
        ).astype(bf16)

    def add_residual(k):
        res_rows = residual.shape[0]

        @pl.when(block(k) == t * res_rows // rows)
        def _():
            own = pl.ds(pl.multiple_of(lax.rem(t * res_rows, rows), res_rows), res_rows)
            total = partial[k, own, :].astype(f32) + residual[...].astype(f32)
            partial[k, own, :] = total.astype(bf16)

    def multiply(k):
        def tile(c, carry):
            multiply_tile(k, c)
            return carry

        lax.fori_loop(0, tiles, tile, 0)
        add_residual(k)

    sets = [(0, 0, 2, early_in, early_out), (1, 2, dp - 2, late_in, late_out)]

    def chunk_at(lane, offset):
        mirrored = place if lane % 2 == 0 else n - place
        index = lax.rem(mirrored + offset + 2 * n, n)
        return pl.ds(pl.multiple_of(index * chunk, chunk), chunk)

    def ring_copy(which, lane, step, src, dst):
        return pltpu.make_async_remote_copy(
            src_ref=src, dst_ref=dst, send_sem=ring_send.at[which, lane, step],
            recv_sem=ring_recv.at[which, lane, step],
            device_id={"tensor": right if lane % 2 == 0 else left}, device_id_type=MESH,
        )

    def sum_copy(group, lane, step):
        which, first, count, arrive, leave = group
        src = leave.at[lane] if step is None else arrive.at[lane, step - 1]
        at = 0 if step is None else step
        return ring_copy(which, lane, at, src, arrive.at[lane, at])

    def arrival(group, lane, step):
        which, first, count, arrive, leave = group
        return ring_copy(which, lane, step, leave.at[lane], arrive.at[lane, step])

    def share_copy(group, lane, step, offset):
        which, first, count, arrive, leave = group
        at = stream.at[pl.ds(first, count), chunk_at(lane, offset), pl.ds(lane * lane_cols, lane_cols)]
        return ring_copy(which, lane, n - 1 + step, at, at)

    def own_part(group, lane, offset):
        which, first, count, arrive, leave = group
        return partial[pl.ds(first, count), chunk_at(lane, offset), pl.ds(lane * lane_cols, lane_cols)]

    def begin(group):
        for lane in range(lanes):
            group[4][lane] = own_part(group, lane, 0)
            sum_copy(group, lane, None).start()

    def add_step(group, step):
        for lane in range(lanes):
            arrival(group, lane, step - 1).wait_recv()
            total = group[3][lane, step - 1].astype(f32) + own_part(group, lane, -step).astype(f32)
            group[3][lane, step - 1] = total.astype(bf16)
            sum_copy(group, lane, step).start()

    def turn(group):
        which, first, count, arrive, leave = group
        for lane in range(lanes):
            arrival(group, lane, n - 2).wait_recv()
            total = arrive[lane, n - 2].astype(f32) + own_part(group, lane, 1).astype(f32)
            cols = pl.ds(lane * lane_cols, lane_cols)
            stream[pl.ds(first, count), chunk_at(lane, 1), cols] = total.astype(bf16)
            share_copy(group, lane, 0, 1).start()

    def share_step(group, step):
        for lane in range(lanes):
            share_copy(group, lane, step - 1, 1 - step).wait_recv()
            share_copy(group, lane, step, 1 - step).start()

    def finish(group):
        for lane in range(lanes):
            share_copy(group, lane, n - 2, 2 - n).wait_recv()

    def sent(group):
        for lane in range(lanes):

            def wait(step, carry):
                arrival(group, lane, step).wait_send()
                share_copy(group, lane, step, 1 - step).wait_send()
                return carry

            lax.fori_loop(0, n - 1, wait, 0)

    def result_copy(k):
        return pltpu.make_async_copy(stream.at[k], stream_out.at[block_rows(k)], out_sem.at[k])

    def block_sums(k):
        for seq in range(rows // LEN):
            at = slice(seq * LEN, (seq + 1) * LEN)
            squares = jnp.zeros((LEN, 128), f32)
            product = jnp.zeros((LEN, 128), f32)
            for c in range(wide // 128):
                cols = slice(c * 128, (c + 1) * 128)
                value = stream[k, at, cols].astype(f32)
                squares += value * value
                product += value * w[:, cols]
            sums[d, block(k), 0, seq : seq + 1, :] = jnp.sum(squares.T, 0, keepdims=True)
            sums[d, block(k), 1, seq : seq + 1, :] = jnp.sum(product.T, 0, keepdims=True)

    def sums_copy(j, source):
        return pltpu.make_async_remote_copy(
            src_ref=sums.at[d], dst_ref=sums.at[source], send_sem=sums_send.at[j - 1],
            recv_sem=sums_recv.at[j - 1], device_id={"dp": lax.rem(d + j, dp)}, device_id_type=MESH,
        )

    units = hid.shape[1] // 128
    per_step = -(-units // (n - 2))

    def turn_unit(i):
        @pl.when(i < units)
        def _():
            cols = pl.ds(pl.multiple_of(i * 128, 128), 128)
            hid_t[cols, :] = hid[:, cols].T

    early, late = sets
    own_copy.wait()
    multiply(0)
    block_wait(1)
    multiply(1)
    begin(early)

    def early_sums(step, carry):
        add_step(early, step)
        return carry

    def early_sums_and_tiles(step, carry):
        add_step(early, step)

        def tile(j, inner):
            i = (step - middle) * tiles_per_step + j

            @pl.when(i < late_tiles)
            def _():
                multiply_tile(2 + i // tiles, lax.rem(i, tiles))

            return inner

        lax.fori_loop(0, tiles_per_step, tile, 0)
        return carry

    first, middle = (n - 1) // 3, (n - 1) // 3 + 2
    late_tiles = (dp - 2) * tiles
    tiles_per_step = -(-late_tiles // (n - 1 - middle))
    lax.fori_loop(1, first + 1, early_sums, 0)
    for k in range(2, dp, 2):
        block_wait(k)
        block_copy(k + 1).start()
    lax.fori_loop(first + 1, middle, early_sums, 0)
    for k in range(3, dp, 2):
        block_wait(k)
    lax.fori_loop(middle, n - 1, early_sums_and_tiles, 0)
    turn(early)
    for k in range(2, dp):
        add_residual(k)
    hid_copy = pltpu.make_async_copy(hid_t, hid_out, out_sem.at[dp])
    begin(late)

    def both(step, carry):
        share_step(early, step)
        add_step(late, step)
        for j in range(per_step):
            turn_unit((step - 1) * per_step + j)
        return carry

    lax.fori_loop(1, n - 1, both, 0)
    finish(early)
    turn(late)
    hid_copy.start()
    for k in range(2):
        result_copy(k).start()
        block_sums(k)

    def late_shares(step, carry):
        share_step(late, step)
        return carry

    lax.fori_loop(1, n - 1, late_shares, 0)
    finish(late)
    for k in range(2, dp):
        result_copy(k).start()
        block_sums(k)
    for j in range(1, dp):
        sums_copy(j, d).start()
    for k in range(1, dp):
        block_copy(k).wait_send()
    sent(early)
    sent(late)
    for j in range(1, dp):
        sums_copy(j, lax.rem(d - j + dp, dp)).wait_recv()
    total = sums[0]
    for source in range(1, dp):
        total += sums[source]
    sums_out[...] = total
    for j in range(1, dp):
        sums_copy(j, d).wait_send()
    for k in range(dp):
        result_copy(k).wait()
    hid_copy.wait()


def stage_rows(depth):
    return 128 if depth % 128 == 0 else depth


def forward(dp, n, hidden, residual, w, master):
    rows, depth = hidden.shape
    wide = master.shape[1]
    tokens = rows * dp
    lanes = 4
    chunk, lane_cols = rows // n, wide // lanes
    bf16 = jnp.bfloat16
    slots = lambda count: pltpu.VMEM((lanes, n - 1, count, chunk, lane_cols), bf16)
    first_slot = lambda count: pltpu.VMEM((lanes, count, chunk, lane_cols), bf16)
    dma = pltpu.SemaphoreType.DMA
    vmem = pl.BlockSpec(memory_space=pltpu.VMEM)
    hbm = pl.BlockSpec(memory_space=pl.ANY)
    return pl.pallas_call(
        functools.partial(forward_kernel, dp, n, lanes),
        in_specs=[vmem, vmem, vmem, hbm],
        out_specs=[hbm, hbm, vmem],
        out_shape=[
            jax.ShapeDtypeStruct((depth, tokens), bf16),
            jax.ShapeDtypeStruct((tokens, wide), bf16),
            jax.ShapeDtypeStruct((dp, 2, rows // LEN, LEN), jnp.float32),
        ],
        scratch_shapes=[
            pltpu.VMEM((tokens, depth), bf16),
            pltpu.VMEM((depth, tokens), bf16),
            pltpu.VMEM((dp, rows, wide), bf16),
            pltpu.VMEM((dp, rows, wide), bf16),
            pltpu.VMEM((dp, dp, 2, rows // LEN, LEN), jnp.float32),
            pltpu.VMEM((3, stage_rows(depth), wide), jnp.float32),
            pltpu.VMEM((depth, wide), bf16),
            slots(2), first_slot(2), slots(dp - 2), first_slot(dp - 2),
            dma((3,)),
            dma,
            dma((dp - 1,)), dma((dp - 1,)),
            dma((2, lanes, 2 * n - 2)), dma((2, lanes, 2 * n - 2)),
            dma((dp - 1,)), dma((dp - 1,)),
            dma((dp + 1,)),
        ],
        compiler_params=pltpu.CompilerParams(
            collective_id=0, has_side_effects=True, vmem_limit_bytes=34 * MIB
        ),
        cost_estimate=pl.CostEstimate(
            flops=2 * tokens * depth * wide, bytes_accessed=4 * depth * wide + 4 * tokens * depth,
            transcendentals=0,
        ),
    )(hidden, residual, w, master)


def per_device(dp, tensor, hidden, residual, master, moment, second, gain, head, lengths, labels):
    w = (gain * head)[None, :]
    hidden_t, stream, sums = forward(dp, tensor, hidden, residual, w, master)
    squares, product = sums[:, 0].reshape(-1, LEN), sums[:, 1].reshape(-1, LEN)
    a, b, loss = row_terms(squares, product, lengths, labels, w.shape[1] * dp)
    new_master, new_moment, new_second = update(
        hidden_t, stream, a, b, w, master, moment, second
    )
    return new_master, new_moment, new_second, loss


def solution(mesh):
    state = P("tensor", "dp")
    return jax.shard_map(
        functools.partial(per_device, mesh.shape["dp"], mesh.shape["tensor"]),
        mesh=mesh,
        in_specs=(P("dp", "tensor"), state, state, state, state, P("dp"), P("dp"), P(), P()),
        out_specs=(state, state, state, P()),
        check_vma=False,
    )
```
